32 devices in a mesh: leaf: 32 (over z, y, x, core).
Axes of the slice: x: 2, y: 2, z: 4, core: 2. Of those that a mesh axis runs over, the one named last changes fastest.
Arguments:
- density: bfloat16 [32768, 220], P('leaf'), may hold values from -6 to 6
- vel_mask: int32 [32768], P('leaf'), may hold values from 0 to 1, as said below
- near_list: int32 [32768, 27], P('leaf'), may hold values from 0 to 32767, as said below
- near_ops: bfloat16 [27, 220, 660], replicated, may hold values from -0.078125 to 0.078125
- upward_ops: bfloat16 [8, 220, 56], replicated, may hold values from -0.0068359375 to 0.0068359375
- coupling_operators: float32 [56, 168], replicated, may hold values from -0.75 to 0.75
- coarse_weights: float32 [8, 8], replicated, may hold values from -2 to 2
- downward_ops: bfloat16 [8, 56, 220], replicated, may hold values from -0.75 to 0.75
- conc_owner: int32 [32768, 1], P('leaf'), may hold values from 0 to 31; in each aligned block of 1024 rows (0 to 1023, 1024 to 2047, ...) at most 64 rows name the same one
- concentration: bfloat16 [65536, 220], P('leaf'), may hold values from -6 to 6
- departure: int32 [65536], P('leaf'), may hold values from 0 to 2047
- departure_class: int32 [65536], P('leaf'), may hold values from 0 to 7
- shift_ops: bfloat16 [8, 220, 220], replicated, may hold values from -0.4375 to 0.4375
- eval_ops: bfloat16 [220, 1024], replicated, may hold values from -0.4375 to 0.4375
Outputs:
- velocity: bfloat16 [32768, 660], P('leaf')
- advected: bfloat16 [65536, 256], P('leaf')
The draws below stay inside these ranges and needn't reach their ends.
Inputs may be any that keep to these rules, and one draw needn't show every extreme that they name: `vel_mask`: in each aligned block of 1024 rows the real leaves come first; every block has from 341 to 1024 real leaves, and both counts occur in every draw. `near_list`: entry [i, t] lies within 1024 of i; column 13 is i itself. `conc_owner`: in each aligned block of 1024 rows, the rows of one device, no owner is named more than 64 times, a bound that some block reaches. `departure`: A slot index within the same device's 2048 slots.
All inputs are finite; a program needn't handle non-finite values.
Results may differ from the reference program's by a relative error of at most 0.008.
Values may be sent and summed in bfloat16 or wider, within the bound.
A program may use at most 128 MiB of HBM per device.

```python
import math
import jax
import jax.numpy as jnp
import numpy as np
from jax import lax

P_SIZE = 220
Q = 56
NEAR = 27
NODES = 256
NCLS = 8
SPAN = 4
L_DEV = 1024
LEAVES = 32768
CAP = 64
SLOTS_DEV = 2048
SLOTS = 65536
NC = 8
BOX_LEAVES = 4096
N_LEAF = 32


def draw_vel_mask(key, part):
    blocks = LEAVES // L_DEV
    first_key, second_key = jax.random.split(jax.random.fold_in(key, 11))
    counts = jax.random.randint(first_key, (blocks,), L_DEV // 3, L_DEV + 1, dtype=jnp.int32)
    shuffled = jax.random.permutation(second_key, blocks)
    counts = counts.at[shuffled[0]].set(L_DEV).at[shuffled[1]].set(L_DEV // 3)
    point_location = jnp.arange(LEAVES, dtype=jnp.int32)
    return (point_location % L_DEV < counts[point_location // L_DEV]).astype(jnp.int32)


def draw_near_list(key, part):
    offsets = jax.random.randint(jax.random.fold_in(key, 23), (LEAVES, NEAR), -L_DEV, L_DEV + 1, dtype=jnp.int32)
    offsets = offsets.at[:, NEAR // 2].set(0)
    point_location = jnp.arange(LEAVES, dtype=jnp.int32)
    return jnp.clip(point_location[:, None] + offsets, 0, LEAVES - 1).astype(jnp.int32)


def with_ends(entries, stream_key, smallest, top_value):
    dims = entries.shape
    index_at = [jax.random.randint(jax.random.fold_in(stream_key, axis), (), 0, dims[axis]) for axis in range(len(dims))]
    entries = entries.at[tuple(index_at)].set(smallest)
    longest = dims.index(max(dims))
    index_at[longest] = (index_at[longest] + 1) % dims[longest]
    return entries.at[tuple(index_at)].set(top_value)


def shard_levels(rng, extent, shards, low, top_value):
    level = 1.0
    for dim, blocks in shards:
        steps = jax.random.uniform(jax.random.fold_in(jax.random.fold_in(rng, 6), dim), (blocks,), jnp.float32, low / len(shards), top_value / len(shards))
        level = level * jnp.repeat(jnp.exp(steps), extent[dim] // blocks).reshape((-1,) + (1,) * (len(extent) - 1 - dim))
    return level


def routed_block(stream_key, own, number, rows, amount, top, limit, skew):
    ranking = jax.random.permutation(stream_key, amount)
    crowded, ordinary = shares(amount, rows * top, limit, skew, True), shares(amount, rows * top, limit, skew, False)
    places = jnp.arange(amount)

    def named(sizes, turn):
        used = int((sizes > 0).sum())
        fixed = max(1, used // 4)
        passed = fixed + (places - fixed + turn * (used - fixed)) % max(1, amount - fixed)
        return jnp.zeros((amount,), jnp.int32).at[ranking[jnp.where(places < fixed, places, passed)]].set(jnp.asarray(sizes, jnp.int32))

    sizes = jnp.where(number % 4 == 0, named(crowded, number // 4), named(ordinary, number - number // 4 - 1))
    mixed = jax.random.permutation(jax.random.fold_in(own, 3), amount)
    giver, taker = mixed[0:amount // 2 * 2:2], mixed[1:amount // 2 * 2:2]
    slack = jnp.minimum(sizes[giver] - 1, limit - sizes[taker]) // 2
    slack = jnp.where((giver == ranking[0]) | (taker == ranking[0]) | (sizes[taker] == 0), 0, jnp.maximum(slack, 0))
    passed = jax.random.randint(jax.random.fold_in(own, 4), (amount // 2,), 0, 1 << 20) % (slack + 1)
    sizes = sizes.at[giver].add(-passed).at[taker].add(passed)
    items = jnp.searchsorted(jnp.cumsum(sizes), jnp.arange(rows * top), side="right").astype(jnp.int32)
    grid = items.reshape(top, rows).T
    grid = grid[jax.random.permutation(jax.random.fold_in(own, 1), rows)]
    turn = jax.random.randint(jax.random.fold_in(own, 2), (rows, 1), 0, top)
    return jnp.take_along_axis(grid, (jnp.arange(top)[None, :] + turn) % top, axis=1)


def shares(number_of, total, limit, lean, full):
    loads = [(1 << 20) // math.isqrt(grade ** lean) + 1 for grade in range(1, number_of + 1)]
    largest = limit if full else min(limit, max(-(-total // number_of), total * loads[0] // sum(loads)))
    least = 1 if total - largest >= number_of - 1 else 0
    given, spare = [largest] + [least] * (number_of - 1), total - largest - least * (number_of - 1)
    while spare > 0:
        free = [i for i in range(1, number_of) if given[i] < largest] or [i for i in range(1, number_of) if given[i] < limit]
        pool, left = sum([loads[i] for i in free]), spare
        for i in free:
            extra = min(limit - given[i], max(1, left * loads[i] // pool), spare)
            given[i] = given[i] + extra
            spare = spare - extra
    return np.array(given)


def normal_values(key, shape, width, bound, pieces=(), kind=jnp.bfloat16):
    values = width * jax.random.normal(key, shape, jnp.float32)
    if pieces:
        values = values * shard_levels(key, shape, pieces, -0.22, 0.18)
    return jnp.clip(values, -bound, bound).astype(kind)


def setup_inputs(seed: int = 0) -> dict:
    key_of = jax.random.split(jax.random.key(seed), 15)
    density = normal_values(key_of[0], (LEAVES, P_SIZE), 1.0, 6.0, ((0, 32),))
    vel_mask = draw_vel_mask(jax.random.fold_in(key_of[14], 71), 0)
    near_list = draw_near_list(jax.random.fold_in(key_of[14], 71), 0)
    near_ops = normal_values(key_of[3], (NEAR, P_SIZE, 3 * P_SIZE), (NEAR * P_SIZE) ** -0.5, 0.078125)
    upward_ops = normal_values(key_of[4], (8, P_SIZE, Q), (P_SIZE * BOX_LEAVES) ** -0.5, 0.0068359375)
    coupling_operators = normal_values(key_of[5], (Q, 3 * Q), Q ** -0.5, 0.75, (), jnp.float32)
    coarse_weights = normal_values(key_of[6], (NC, NC), NC ** -0.5, 2.0, (), jnp.float32)
    downward_ops = normal_values(key_of[7], (8, Q, P_SIZE), Q ** -0.5, 0.75)
    conc_owner_keys = jax.random.split(jax.random.fold_in(key_of[8], 1), LEAVES // L_DEV)
    conc_owner_turns = jax.random.permutation(jax.random.fold_in(key_of[8], 3), LEAVES // L_DEV)
    conc_owner = jax.vmap(lambda own, number: routed_block(jax.random.fold_in(key_of[8], 2), own, number, L_DEV, N_LEAF, 1, CAP, 2))(conc_owner_keys, conc_owner_turns).reshape((LEAVES, 1))
    concentration = normal_values(key_of[9], (SLOTS, P_SIZE), 1.0, 6.0, ((0, 32),))
    departure = with_ends(jax.random.randint(key_of[10], (SLOTS,), 0, SLOTS_DEV), jax.random.fold_in(key_of[10], 1), 0, SLOTS_DEV - 1).astype(jnp.int32)
    departure_class = with_ends(jax.random.randint(key_of[11], (SLOTS,), 0, NCLS), jax.random.fold_in(key_of[11], 1), 0, NCLS - 1).astype(jnp.int32)
    shift_ops = normal_values(key_of[12], (NCLS, P_SIZE, P_SIZE), P_SIZE ** -0.5, 0.4375)
    eval_ops = normal_values(key_of[13], (P_SIZE, 4 * NODES), P_SIZE ** -0.5, 0.4375)
    return {"density": density, "vel_mask": vel_mask, "near_list": near_list, "near_ops": near_ops, "upward_ops": upward_ops, "coupling_operators": coupling_operators, "coarse_weights": coarse_weights, "downward_ops": downward_ops, "conc_owner": conc_owner, "concentration": concentration, "departure": departure, "departure_class": departure_class, "shift_ops": shift_ops, "eval_ops": eval_ops}


time_step = 0.5


def shifted_rows(gathered, classes, shift_ops):
    stacked_rows = jnp.einsum('rk,tkm->trm', gathered.astype(jnp.float32), shift_ops.astype(jnp.float32))
    select = (classes[None, :] == jnp.arange(shift_ops.shape[0], dtype=jnp.int32)[:, None]).astype(jnp.float32)
    return jnp.sum(stacked_rows * select[:, :, None], axis=0).astype(jnp.bfloat16)


def advect_rows(base, velocity_rows, alive_rows, eval_ops):
    eval_wide = eval_ops.astype(jnp.float32)
    value_rows = jnp.dot(base.astype(jnp.float32), eval_wide)
    nodes_count = value_rows.shape[1] // 4
    speeds = jnp.dot(velocity_rows.reshape(-1, eval_ops.shape[0]).astype(jnp.float32), eval_wide[:, :nodes_count])
    speeds = speeds.reshape(base.shape[0], 3, nodes_count)
    correction = speeds[:, 0] * value_rows[:, nodes_count:2 * nodes_count]
    correction = correction + speeds[:, 1] * value_rows[:, 2 * nodes_count:3 * nodes_count]
    correction = correction + speeds[:, 2] * value_rows[:, 3 * nodes_count:]
    return (alive_rows[:, None] * (value_rows[:, :nodes_count] - time_step * correction)).astype(jnp.bfloat16)


def reference(density, vel_mask, near_list, near_ops, upward_ops, coupling_operators, coarse_weights, downward_ops, conc_owner, concentration, departure, departure_class, shift_ops, eval_ops):
    leaves_all = density.shape[0]
    blocks = leaves_all // L_DEV
    alive = vel_mask.astype(jnp.float32)
    live_density = (density.astype(jnp.float32) * alive[:, None]).astype(jnp.bfloat16)
    parts = jnp.einsum('gop,opq->goq', live_density.reshape(-1, 8, P_SIZE).astype(jnp.float32), upward_ops.astype(jnp.float32))
    moments = jnp.sum(parts.reshape(NC, BOX_LEAVES // 8, 8, Q), axis=(1, 2))
    expanded = jnp.dot(moments, coupling_operators, precision=lax.Precision.HIGHEST)
    local_expansion = jnp.dot(coarse_weights, expanded, precision=lax.Precision.HIGHEST)
    far_all = jnp.einsum('cjq,oqp->cojp', local_expansion.reshape(NC, 3, Q), downward_ops.astype(jnp.float32), precision=lax.Precision.HIGHEST)
    flat_ops = near_ops.reshape(NEAR * P_SIZE, 3 * P_SIZE).astype(jnp.float32)

    def one_block(index):
        rows = lax.dynamic_slice_in_dim(near_list, index * L_DEV, L_DEV, 0)
        gathered = live_density[rows].reshape(L_DEV, NEAR * P_SIZE).astype(jnp.float32)
        nearby_field = jnp.dot(gathered, flat_ops)
        box_far = far_all[index // SPAN].reshape(1, 8, 3 * P_SIZE)
        far_field = jnp.broadcast_to(box_far, (L_DEV // 8, 8, 3 * P_SIZE)).reshape(L_DEV, 3 * P_SIZE)
        alive_rows = lax.dynamic_slice_in_dim(alive, index * L_DEV, L_DEV, 0)
        return ((nearby_field + far_field) * alive_rows[:, None]).astype(jnp.bfloat16)

    velocity = lax.map(one_block, jnp.arange(blocks, dtype=jnp.int32)).reshape(leaves_all, 3 * P_SIZE)
    owner = conc_owner[:, 0].reshape(blocks, L_DEV)
    onehot = (owner[:, :, None] == jnp.arange(N_LEAF, dtype=jnp.int32)[None, None, :]).astype(jnp.int32)
    rank = jnp.sum(jnp.cumsum(onehot, axis=1) * onehot, axis=2) - 1
    capacity = SLOTS_DEV // N_LEAF
    slot = owner * SLOTS_DEV + jnp.arange(blocks, dtype=jnp.int32)[:, None] * capacity + rank
    slot = slot.reshape(leaves_all).astype(jnp.int32)
    received_velocity = jnp.zeros((SLOTS, 3 * P_SIZE), jnp.bfloat16).at[slot].set(velocity)
    filled = jnp.zeros((SLOTS,), jnp.float32).at[slot].set(alive)

    def one_device(index):
        start = index * SLOTS_DEV
        conc_rows = lax.dynamic_slice_in_dim(concentration, start, SLOTS_DEV, 0)
        depart_rows = lax.dynamic_slice_in_dim(departure, start, SLOTS_DEV, 0)
        class_rows = lax.dynamic_slice_in_dim(departure_class, start, SLOTS_DEV, 0)
        base = shifted_rows(conc_rows[depart_rows], class_rows, shift_ops)
        velocity_rows = lax.dynamic_slice_in_dim(received_velocity, start, SLOTS_DEV, 0)
        alive_rows = lax.dynamic_slice_in_dim(filled, start, SLOTS_DEV, 0)
        return advect_rows(base, velocity_rows, alive_rows, eval_ops)

    advected = lax.map(one_device, jnp.arange(N_LEAF, dtype=jnp.int32)).reshape(SLOTS, NODES)
    return velocity, advected
```

```python
import functools

import jax
import jax.numpy as jnp
from jax import lax
from jax.experimental import pallas as pl
from jax.experimental.pallas import tpu as pltpu
from jax.sharding import PartitionSpec as P

SPAN = 4


time_step = 0.5


LANES = 128


def halo(block):
    count = lax.axis_size("leaf")
    forward = [(i, i + 1) for i in range(count - 1)]
    backward = [(target, source) for source, target in forward]
    return lax.ppermute(block, "leaf", forward), lax.ppermute(block, "leaf", backward)


def near_kernel(rows, group, idx_ref, low_ref, mid_ref, high_ref, ops_ref, out_ref, source, picked, lhs, weights):
    block = pl.program_id(0)
    taps, depth, _ = ops_ref.shape
    wide = 2 * LANES
    leaves = mid_ref.shape[0]

    @pl.when(block == 0)
    def _():
        for part, ref in enumerate((low_ref, mid_ref, high_ref)):
            @pl.loop(0, leaves // rows)
            def _(chunk):
                values = ref[pl.ds(chunk * rows, rows), :].astype(jnp.float32)
                at = 2 * (part * leaves + chunk * rows)
                source[pl.ds(at, rows, stride=2), :] = values[:, :LANES]
                source[pl.ds(at + 1, rows, stride=2), :] = values[:, LANES:]

        @pl.loop(0, taps)
        def _(tap):
            at = pl.multiple_of(tap * wide, wide)
            weights[pl.ds(at, wide), :] = jnp.concatenate(
                [ops_ref[tap], jnp.zeros((wide - depth, ops_ref.shape[2]), ops_ref.dtype)], axis=0
            )

    count = group * rows

    def pick(turn):
        at = (block * (taps // group) + turn) * count
        for r in range(count):
            row = pl.multiple_of(idx_ref[at + r], 2)
            picked[pl.ds(2 * r, 2), :] = source[pl.ds(row, 2), :]

    def settle():
        for j in range(group):
            for half in range(2):
                values = picked[pl.ds(2 * j * rows + half, rows, stride=2), :]
                lhs[:, (2 * j + half) * LANES : (2 * j + half + 1) * LANES] = values.astype(jnp.bfloat16)

    def product(turn):
        at = pl.multiple_of(turn * (group * wide), group * wide)
        return jnp.dot(lhs[...], weights[pl.ds(at, group * wide), :], preferred_element_type=jnp.float32)

    out_ref[...] = jnp.zeros_like(out_ref)
    pick(0)
    settle()

    @pl.loop(0, taps // group - 1)
    def _(turn):
        out_ref[...] += product(turn)
        pick(turn + 1)
        settle()

    out_ref[...] += product(taps // group - 1)


def near_field(low, mid, high, local_rows, near_ops):
    leaves = mid.shape[0]
    taps, _, outs = near_ops.shape
    rows = 256 if leaves % 256 == 0 else leaves
    group = 3 if taps % 3 == 0 else 1
    flat = (2 * local_rows).reshape(leaves // rows, rows, taps).transpose(0, 2, 1).reshape(-1)
    vmem = pl.BlockSpec(memory_space=pltpu.VMEM)
    return pl.pallas_call(
        functools.partial(near_kernel, rows, group),
        out_shape=jax.ShapeDtypeStruct((leaves, outs), jnp.float32),
        grid=(leaves // rows,),
        in_specs=[pl.BlockSpec(memory_space=pltpu.SMEM), vmem, vmem, vmem, vmem],
        out_specs=pl.BlockSpec((rows, outs), lambda i: (i, 0)),
        scratch_shapes=[
            pltpu.VMEM((6 * leaves, LANES), jnp.float32),
            pltpu.VMEM((2 * group * rows, LANES), jnp.float32),
            pltpu.VMEM((rows, group * 2 * LANES), jnp.bfloat16),
            pltpu.VMEM((taps * 2 * LANES, outs), jnp.bfloat16),
        ],
        compiler_params=pltpu.CompilerParams(
            dimension_semantics=("arbitrary",), vmem_limit_bytes=48 * 1024 * 1024
        ),
        cost_estimate=pl.CostEstimate(
            flops=2 * leaves * taps * 2 * LANES * outs * 5, bytes_accessed=100_000_000, transcendentals=0
        ),
        name="near_field",
    )(flat, low, mid, high, near_ops)


def split3(values):
    high = values.astype(jnp.bfloat16)
    rest = values - high.astype(jnp.float32)
    middle = rest.astype(jnp.bfloat16)
    return jnp.stack([high, middle, (rest - middle.astype(jnp.float32)).astype(jnp.bfloat16)], axis=-1)


def shifted_rows(gathered, classes, shift_ops):
    kinds = shift_ops.shape[0]
    total = jnp.zeros((gathered.shape[0], shift_ops.shape[2]), jnp.float32)
    for kind in range(kinds):
        product = jnp.dot(gathered, shift_ops[kind], preferred_element_type=jnp.float32)
        total = jnp.where((classes == kind)[:, None], product, total)
    return total.astype(jnp.bfloat16)


def advect_rows(base, velocity_rows, alive_rows, eval_ops):
    value_rows = jnp.dot(base, eval_ops, preferred_element_type=jnp.float32)
    nodes_count = value_rows.shape[1] // 4
    speeds = jnp.dot(
        velocity_rows.reshape(-1, eval_ops.shape[0]),
        eval_ops[:, :nodes_count],
        preferred_element_type=jnp.float32,
    )
    speeds = speeds.reshape(base.shape[0], 3, nodes_count)
    correction = speeds[:, 0] * value_rows[:, nodes_count : 2 * nodes_count]
    correction = correction + speeds[:, 1] * value_rows[:, 2 * nodes_count : 3 * nodes_count]
    correction = correction + speeds[:, 2] * value_rows[:, 3 * nodes_count :]
    return (alive_rows[:, None] * (value_rows[:, :nodes_count] - time_step * correction)).astype(
        jnp.bfloat16
    )


def local(
    density,
    vel_mask,
    near_list,
    near_ops,
    upward_ops,
    coupling_operators,
    coarse_weights,
    downward_ops,
    conc_owner,
    concentration,
    departure,
    departure_class,
    shift_ops,
    eval_ops,
):
    leaves = density.shape[0]
    coef_width = density.shape[1]
    devices = lax.axis_size("leaf")
    my_index = lax.axis_index("leaf")
    alive = vel_mask.astype(jnp.float32)
    live_density = (density.astype(jnp.float32) * alive[:, None]).astype(jnp.bfloat16)
    wide = jnp.pad(live_density, ((0, 0), (0, 2 * LANES - coef_width)))
    low, high = halo(wide)
    local_rows = near_list - my_index * leaves + leaves
    nearby_field = near_field(low, wide, high, local_rows, near_ops)
    parts = jnp.einsum(
        "gop,opq->goq",
        live_density.reshape(-1, 8, coef_width),
        upward_ops,
        preferred_element_type=jnp.float32,
    )
    own_part = jnp.sum(parts, axis=(0, 1))
    slots_here = concentration.shape[0]
    capacity = slots_here // devices
    base = shifted_rows(concentration[departure], departure_class, shift_ops)
    densities = own_part.shape[0]
    columns = -(-densities // capacity)
    carried = split3(jnp.pad(own_part, (0, columns * capacity - densities)))
    carried = jnp.broadcast_to(
        carried.reshape(1, capacity, 3 * columns), (devices, capacity, 3 * columns)
    )
    got = lax.all_to_all(
        jnp.concatenate([base.reshape(devices, capacity, coef_width), carried], axis=2),
        "leaf",
        split_axis=0,
        concat_axis=0,
        tiled=True,
    )
    got_base = got[:, :, :coef_width]
    all_parts = jnp.sum(
        got[:, :, coef_width:].astype(jnp.float32).reshape(devices, columns * capacity, 3), axis=2
    )[:, :densities]
    moments = jnp.sum(all_parts.reshape(devices // SPAN, SPAN, densities), axis=1)
    my_box = my_index // SPAN
    expanded = jnp.dot(moments, coupling_operators, precision=lax.Precision.HIGHEST)
    weight_row = lax.dynamic_slice_in_dim(coarse_weights, my_box, 1, 0)
    own_expansion = jnp.dot(weight_row, expanded, precision=lax.Precision.HIGHEST)
    box_far = jnp.einsum(
        "jq,oqp->ojp",
        own_expansion.reshape(3, -1),
        downward_ops.astype(jnp.float32),
        precision=lax.Precision.HIGHEST,
    )
    far_field = jnp.broadcast_to(
        box_far.reshape(1, 8, 3 * coef_width), (leaves // 8, 8, 3 * coef_width)
    ).reshape(leaves, 3 * coef_width)
    velocity = ((nearby_field + far_field) * alive[:, None]).astype(jnp.bfloat16)
    owner = conc_owner[:, 0]
    onehot = owner[:, None] == jnp.arange(devices, dtype=jnp.int32)[None, :]
    order = jnp.arange(leaves, dtype=jnp.int32)
    earlier = (order[None, :] < order[:, None]).astype(jnp.bfloat16)
    before = jnp.dot(earlier, onehot.astype(jnp.bfloat16), preferred_element_type=jnp.float32)
    rank = jnp.sum(jnp.where(onehot, before, 0.0), axis=1).astype(jnp.int32)
    send_slot = owner * capacity + rank
    placement = (jnp.arange(slots_here, dtype=jnp.int32)[:, None] == send_slot[None, :]).astype(
        jnp.bfloat16
    )
    send_velocity = jnp.dot(placement, velocity, preferred_element_type=jnp.float32).astype(
        jnp.bfloat16
    )
    send_alive = jnp.dot(
        placement, vel_mask.astype(jnp.bfloat16), preferred_element_type=jnp.float32
    ).astype(jnp.bfloat16)
    result = advect_rows(
        got_base.reshape(slots_here, -1), send_velocity, send_alive.astype(jnp.float32), eval_ops
    )
    returned = lax.all_to_all(
        result.reshape(devices, capacity, -1), "leaf", split_axis=0, concat_axis=0, tiled=True
    )
    advected = returned.reshape(slots_here, -1)
    return (velocity, advected)


def solution(mesh):
    placed = (
        P("leaf", None),
        P("leaf"),
        P("leaf", None),
        P(),
        P(),
        P(),
        P(),
        P(),
        P("leaf", None),
        P("leaf", None),
        P("leaf"),
        P("leaf"),
        P(),
        P(),
    )
    return jax.shard_map(
        local,
        mesh=mesh,
        in_specs=placed,
        out_specs=(P("leaf", None), P("leaf", None)),
        check_vma=False,
    )
```

```python
import functools

import jax
import jax.numpy as jnp
from jax import lax
from jax.experimental import pallas as pl
from jax.experimental.pallas import tpu as pltpu
from jax.sharding import PartitionSpec as P

SPAN = 4


time_step = 0.5


LANES = 128


def halo(block):
    count = lax.axis_size("leaf")
    forward = [(i, i + 1) for i in range(count - 1)]
    backward = [(target, source) for source, target in forward]
    return lax.ppermute(block, "leaf", forward), lax.ppermute(block, "leaf", backward)


def lane_halves(target, at, values):
    count, width = values.shape
    target[pl.ds(at, count, stride=2), :] = values[:, :LANES]
    upper = values[:, LANES:]
    if width < 2 * LANES:
        upper = jnp.concatenate([upper, jnp.zeros((count, 2 * LANES - width), values.dtype)], axis=1)
    target[pl.ds(at + 1, count, stride=2), :] = upper


def near_kernel(rows, group, idx_ref, low_ref, mid_ref, high_ref, ops_ref, out_ref, source, picked, lhs, raw, weights, sem):
    block = pl.program_id(0)
    taps, _, depth = ops_ref.shape
    wide = 2 * LANES
    leaves = mid_ref.shape[0]
    fetch = pltpu.make_async_copy(ops_ref, raw, sem)

    def pick(turn):
        for j in range(group):
            at = (turn * group + j) * leaves + block * rows
            for r in range(rows):
                row = pl.multiple_of(idx_ref[at + r], 2)
                picked[pl.ds(2 * (j * rows + r), 2), :] = source[pl.ds(row, 2), :]

    def settle():
        for j in range(group):
            for half in range(2):
                values = picked[pl.ds(2 * j * rows + half, rows, stride=2), :]
                lhs[:, (2 * j + half) * LANES : (2 * j + half + 1) * LANES] = values.astype(jnp.bfloat16)

    def product(turn):
        at = pl.multiple_of(turn * (group * wide), group * wide)
        return lax.dot_general(
            weights[:, pl.ds(at, group * wide)],
            lhs[...],
            (((1,), (1,)), ((), ())),
            preferred_element_type=jnp.float32,
        )

    @pl.when(block == 0)
    def _():
        fetch.start()
        for part, ref in enumerate((low_ref, mid_ref, high_ref)):
            @pl.loop(0, leaves // rows)
            def _(chunk):
                values = ref[pl.ds(chunk * rows, rows), :].astype(jnp.float32)
                lane_halves(source, 2 * (part * leaves + chunk * rows), values)

    pick(0)
    settle()

    @pl.when(block == 0)
    def _():
        fetch.wait()
        for tap in range(taps):
            weights[:, tap * wide + LANES : (tap + 1) * wide] = jnp.zeros((weights.shape[0], LANES), weights.dtype)
            weights[:, tap * wide : tap * wide + depth] = raw[tap]

    out_ref[...] = jnp.zeros_like(out_ref)

    @pl.loop(0, taps // group - 1)
    def _(turn):
        out_ref[...] += product(turn)
        pick(turn + 1)
        settle()

    out_ref[...] += product(taps // group - 1)


def near_field(low, mid, high, local_rows, near_ops):
    leaves = mid.shape[0]
    taps, depth, outs = near_ops.shape
    rows = 256 if leaves % 256 == 0 else leaves
    group = 3 if taps % 3 == 0 else 1
    flat = (2 * local_rows).T.reshape(-1)
    vmem = pl.BlockSpec(memory_space=pltpu.VMEM)
    return pl.pallas_call(
        functools.partial(near_kernel, rows, group),
        out_shape=jax.ShapeDtypeStruct((outs, leaves), jnp.float32),
        grid=(leaves // rows,),
        in_specs=[
            pl.BlockSpec(memory_space=pltpu.SMEM), vmem, vmem, vmem, pl.BlockSpec(memory_space=pl.ANY)
        ],
        out_specs=pl.BlockSpec((outs, rows), lambda i: (0, i)),
        scratch_shapes=[
            pltpu.VMEM((6 * leaves, LANES), jnp.float32),
            pltpu.VMEM((2 * group * rows, LANES), jnp.float32),
            pltpu.VMEM((rows, group * 2 * LANES), jnp.bfloat16),
            pltpu.VMEM((taps, outs, depth), jnp.bfloat16),
            pltpu.VMEM((outs, taps * 2 * LANES), jnp.bfloat16),
            pltpu.SemaphoreType.DMA(()),
        ],
        compiler_params=pltpu.CompilerParams(
            dimension_semantics=("arbitrary",), vmem_limit_bytes=48 * 1024 * 1024
        ),
        cost_estimate=pl.CostEstimate(
            flops=2 * leaves * taps * 2 * LANES * outs * 5, bytes_accessed=100_000_000, transcendentals=0
        ),
        name="near_field",
    )(flat, low, mid, high, near_ops.transpose(0, 2, 1))


def base_kernel(rows, capacity, idx_ref, field_ref, class_ref, ops_ref, carried_ref, out_ref, source, picked, lhs, weights):
    block = pl.program_id(0)
    kinds, depth, outs = ops_ref.shape
    wide = 2 * LANES

    @pl.when(block == 0)
    def _():
        @pl.loop(0, field_ref.shape[0] // rows)
        def _(chunk):
            values = field_ref[pl.ds(chunk * rows, rows), :].astype(jnp.float32)
            lane_halves(source, 2 * chunk * rows, values)

        for kind in range(kinds):
            weights[kind * wide : (kind + 1) * wide, LANES:] = jnp.zeros((wide, LANES), weights.dtype)
            weights[kind * wide : (kind + 1) * wide, :outs] = jnp.concatenate(
                [ops_ref[kind], jnp.zeros((wide - depth, outs), ops_ref.dtype)], axis=0
            )

    for r in range(rows):
        row = pl.multiple_of(2 * idx_ref[block * rows + r], 2)
        picked[2 * r : 2 * r + 2, :] = source[pl.ds(row, 2), :]
    halves = [picked[pl.ds(half, rows, stride=2), :] for half in range(2)]
    for kind in range(kinds):
        chosen = class_ref[...] == kind
        for half in range(2):
            at = kind * wide + half * LANES
            lhs[:, at : at + LANES] = jnp.where(chosen, halves[half], 0.0).astype(jnp.bfloat16)
    total = jnp.dot(lhs[...], weights[...], preferred_element_type=jnp.float32)
    extra = carried_ref[...].astype(jnp.float32)
    out_ref[...] = (total + jnp.concatenate([extra] * (rows // capacity), axis=0)).astype(jnp.bfloat16)


def base_rows(concentration, departure, departure_class, shift_ops, carried):
    slots, width = concentration.shape
    capacity = carried.shape[0]
    kinds = shift_ops.shape[0]
    rows = 256 if slots % 256 == 0 and 256 % capacity == 0 else slots
    wide = 2 * LANES
    vmem = pl.BlockSpec(memory_space=pltpu.VMEM)
    return pl.pallas_call(
        functools.partial(base_kernel, rows, capacity),
        out_shape=jax.ShapeDtypeStruct((slots, wide), jnp.bfloat16),
        grid=(slots // rows,),
        in_specs=[
            pl.BlockSpec(memory_space=pltpu.SMEM),
            vmem,
            pl.BlockSpec((rows, 1), lambda i: (i, 0)),
            vmem,
            vmem,
        ],
        out_specs=pl.BlockSpec((rows, wide), lambda i: (i, 0)),
        scratch_shapes=[
            pltpu.VMEM((2 * slots, LANES), jnp.float32),
            pltpu.VMEM((2 * rows, LANES), jnp.float32),
            pltpu.VMEM((rows, kinds * wide), jnp.bfloat16),
            pltpu.VMEM((kinds * wide, wide), jnp.bfloat16),
        ],
        compiler_params=pltpu.CompilerParams(
            dimension_semantics=("arbitrary",), vmem_limit_bytes=32 * 1024 * 1024
        ),
        cost_estimate=pl.CostEstimate(
            flops=2 * slots * kinds * wide * wide, bytes_accessed=4 * slots * wide, transcendentals=0
        ),
        name="base_rows",
    )(departure, concentration, departure_class[:, None], shift_ops, carried)


MESH = pl.DeviceIdType.MESH


def return_kernel(
    n, group, slot_ref, alive_ref, near_ref, far_ref, got_ref, eval_ref, vel_ref, adv_ref,
    moved, spread, spread_low, values_op, result, send_sem, recv_sem,
):
    me = lax.axis_index("leaf")
    capacity, wide = got_ref.shape[1], got_ref.shape[2]
    depth, nodes = eval_ref.shape[0], eval_ref.shape[1] // 4
    outs, leaves = near_ref.shape
    padded = moved.shape[0]
    rows = group * capacity
    barrier = pltpu.get_barrier_semaphore()

    @pl.loop(1, n)
    def _(turn):
        pl.semaphore_signal(barrier, inc=1, device_id=(lax.rem(me + turn, n),), device_id_type=MESH)

    far = far_ref[...]
    for at in range(0, leaves, LANES):
        block = ((near_ref[:, at : at + LANES] + far) * alive_ref[:, at : at + LANES]).astype(jnp.bfloat16)
        vel_ref[:, at : at + LANES] = block
        moved[:, at : at + LANES] = jnp.concatenate(
            [block, jnp.ones((padded - outs, LANES), jnp.bfloat16)], axis=0
        )
    spread[...] = jnp.zeros_like(spread)
    for j in range(3):
        spread[j * depth : (j + 1) * depth, j * nodes : (j + 1) * nodes] = eval_ref[:, :nodes].astype(jnp.float32)
    spread_low[...] = spread[...].astype(jnp.bfloat16)
    values_op[...] = jnp.concatenate(
        [eval_ref[...], jnp.zeros((wide - depth, 4 * nodes), jnp.bfloat16)], axis=0
    )
    pl.semaphore_wait(barrier, n - 1)

    def copy(turn, landing):
        return pltpu.make_async_remote_copy(
            src_ref=result.at[turn],
            dst_ref=adv_ref.at[landing],
            send_sem=send_sem.at[turn],
            recv_sem=recv_sem.at[turn],
            device_id=(lax.rem(me + turn, n),),
            device_id_type=MESH,
        )

    @pl.loop(0, n // group)
    def _(step):
        ids = lax.broadcasted_iota(jnp.int32, (rows, 1), 0) + step * rows
        placed = jnp.where(slot_ref[...] == ids, 1.0, 0.0).astype(jnp.bfloat16)
        sent = lax.dot_general(
            placed, moved[...], (((1,), (1,)), ((), ())), preferred_element_type=jnp.float32
        )
        speeds = jnp.dot(sent.astype(jnp.bfloat16), spread_low[...], preferred_element_type=jnp.float32)
        base = jnp.concatenate(
            [got_ref[lax.rem(me + step * group + j, n)] for j in range(group)], axis=0
        )
        values = jnp.dot(base, values_op[...], preferred_element_type=jnp.float32)
        correction = speeds[:, :nodes] * values[:, nodes : 2 * nodes]
        correction = correction + speeds[:, nodes : 2 * nodes] * values[:, 2 * nodes : 3 * nodes]
        correction = correction + speeds[:, 2 * nodes :] * values[:, 3 * nodes :]
        filled = sent[:, outs : outs + 1]
        final = (filled * (values[:, :nodes] - time_step * correction)).astype(jnp.bfloat16)
        for j in range(group):
            result[step * group + j] = final[j * capacity : (j + 1) * capacity]
        for j in range(group):
            if j:
                copy(step * group + j, me).start()
            else:
                @pl.when(step > 0)
                def _():
                    copy(step * group, me).start()

    adv_ref[me] = result[0]

    @pl.loop(1, n)
    def _(turn):
        copy(turn, lax.rem(me - turn + n, n)).wait()


def advect_return(slot, alive, near, far, got, eval_ops):
    n, capacity, wide = got.shape
    depth, columns = eval_ops.shape
    outs, leaves = near.shape
    nodes = columns // 4
    group = 256 // capacity if 256 % capacity == 0 and n % (256 // capacity) == 0 else 1
    padded = -(-(outs + 1) // (2 * LANES)) * (2 * LANES)
    vmem = pl.BlockSpec(memory_space=pltpu.VMEM)
    return pl.pallas_call(
        functools.partial(return_kernel, n, group),
        out_shape=(
            jax.ShapeDtypeStruct((outs, leaves), jnp.bfloat16),
            jax.ShapeDtypeStruct((n, capacity, nodes), jnp.bfloat16),
        ),
        in_specs=[vmem] * 6,
        out_specs=(vmem, vmem),
        scratch_shapes=[
            pltpu.VMEM((padded, leaves), jnp.bfloat16),
            pltpu.VMEM((padded, 3 * nodes), jnp.float32),
            pltpu.VMEM((padded, 3 * nodes), jnp.bfloat16),
            pltpu.VMEM((wide, columns), jnp.bfloat16),
            pltpu.VMEM((n, capacity, nodes), jnp.bfloat16),
            pltpu.SemaphoreType.DMA((n,)),
            pltpu.SemaphoreType.DMA((n,)),
        ],
        compiler_params=pltpu.CompilerParams(
            collective_id=0, has_side_effects=True, vmem_limit_bytes=48 * 1024 * 1024
        ),
        cost_estimate=pl.CostEstimate(
            flops=2 * n * capacity * (leaves * padded + padded * 3 * nodes + wide * columns),
            bytes_accessed=10_000_000,
            transcendentals=0,
        ),
        name="advect_return",
    )(slot, alive, near, far, got, eval_ops)


def rounded(values):
    return lax.reduce_precision(values, exponent_bits=8, mantissa_bits=7)


def split3(values):
    high = rounded(values)
    middle = rounded(values - high)
    low = rounded(values - high - middle)
    return jnp.stack([high, middle, low], axis=-1).astype(jnp.bfloat16)


def local(
    density,
    vel_mask,
    near_list,
    near_ops,
    upward_ops,
    coupling_operators,
    coarse_weights,
    downward_ops,
    conc_owner,
    concentration,
    departure,
    departure_class,
    shift_ops,
    eval_ops,
):
    leaves = density.shape[0]
    coef_width = density.shape[1]
    devices = lax.axis_size("leaf")
    my_index = lax.axis_index("leaf")
    alive = vel_mask.astype(jnp.float32)
    live_density = (density.astype(jnp.float32) * alive[:, None]).astype(jnp.bfloat16)
    wide = jnp.pad(live_density, ((0, 0), (0, 2 * LANES - coef_width)))
    low, high = halo(wide)
    local_rows = near_list - my_index * leaves + leaves
    nearby_field = near_field(low, wide, high, local_rows, near_ops)
    parts = jnp.einsum(
        "gop,opq->goq",
        live_density.reshape(-1, 8, coef_width),
        upward_ops,
        preferred_element_type=jnp.float32,
    )
    own_part = jnp.sum(parts, axis=(0, 1))
    slots_here = concentration.shape[0]
    capacity = slots_here // devices
    densities = own_part.shape[0]
    columns = -(-densities // capacity)
    carried = split3(jnp.pad(own_part, (0, columns * capacity - densities)))
    carried = jnp.pad(
        carried.reshape(capacity, 3 * columns),
        ((0, 0), (coef_width, 2 * LANES - coef_width - 3 * columns)),
    )
    base = base_rows(concentration, departure, departure_class, shift_ops, carried)
    got = lax.all_to_all(
        base.reshape(devices, capacity, -1), "leaf", split_axis=0, concat_axis=0, tiled=True
    )
    all_parts = jnp.sum(
        got[:, :, coef_width : coef_width + 3 * columns]
        .astype(jnp.float32)
        .reshape(devices, columns * capacity, 3),
        axis=2,
    )[:, :densities]
    moments = jnp.sum(all_parts.reshape(devices // SPAN, SPAN, densities), axis=1)
    my_box = my_index // SPAN
    expanded = jnp.dot(moments, coupling_operators, precision=lax.Precision.HIGHEST)
    weight_row = lax.dynamic_slice_in_dim(coarse_weights, my_box, 1, 0)
    own_expansion = jnp.dot(weight_row, expanded, precision=lax.Precision.HIGHEST)
    box_far = jnp.einsum(
        "jq,oqp->jpo",
        own_expansion.reshape(3, -1),
        downward_ops.astype(jnp.float32),
        precision=lax.Precision.HIGHEST,
    )
    far = jnp.tile(box_far.reshape(3 * coef_width, 8), (1, LANES // 8))
    owner = conc_owner[:, 0]
    onehot = owner[:, None] == jnp.arange(devices, dtype=jnp.int32)[None, :]
    order = jnp.arange(leaves, dtype=jnp.int32)
    earlier = (order[None, :] < order[:, None]).astype(jnp.bfloat16)
    before = jnp.dot(earlier, onehot.astype(jnp.bfloat16), preferred_element_type=jnp.float32)
    rank = jnp.sum(jnp.where(onehot, before, 0.0), axis=1).astype(jnp.int32)
    relative = lax.rem(owner - my_index + devices, devices)
    send_slot = jnp.where(vel_mask > 0, relative * capacity + rank, -1)
    velocity, advected = advect_return(
        send_slot[None, :], alive[None, :], nearby_field, far, got, eval_ops
    )
    return (velocity.T, advected.reshape(slots_here, -1))


def solution(mesh):
    placed = (
        P("leaf", None),
        P("leaf"),
        P("leaf", None),
        P(),
        P(),
        P(),
        P(),
        P(),
        P("leaf", None),
        P("leaf", None),
        P("leaf"),
        P("leaf"),
        P(),
        P(),
    )
    return jax.shard_map(
        local,
        mesh=mesh,
        in_specs=placed,
        out_specs=(P("leaf", None), P("leaf", None)),
        check_vma=False,
    )
```

```python
import functools

import jax
import jax.numpy as jnp
from jax import lax
from jax.experimental import pallas as pl
from jax.experimental.pallas import tpu as pltpu
from jax.sharding import PartitionSpec as P

SPAN = 4


time_step = 0.5


LANES = 128


MESH = pl.DeviceIdType.MESH


def lane_halves(target, at, values):
    count, width = values.shape
    target = target.reshape(2 * target.shape[0], LANES)
    target[pl.ds(at, count, stride=2), :] = values[:, :LANES]
    upper = values[:, LANES:]
    if width < 2 * LANES:
        upper = jnp.concatenate([upper, jnp.zeros((count, 2 * LANES - width), values.dtype)], axis=1)
    target[pl.ds(at + 1, count, stride=2), :] = upper


def near_kernel(rows, group, idx_ref, low_ref, mid_ref, high_ref, ops_ref, out_ref, source, picked, lhs, weights):
    block = pl.program_id(0)
    taps, _, depth = ops_ref.shape
    wide = 2 * LANES
    leaves = mid_ref.shape[0]

    def pick(turn):
        for j in range(group):
            at = (turn * group + j) * leaves + block * rows
            for r in range(rows):
                picked[j * rows + r] = source[idx_ref[at + r]]

    def settle():
        flat = picked.reshape(2 * group * rows, LANES)
        for j in range(group):
            for half in range(2):
                values = flat[pl.ds(2 * j * rows + half, rows, stride=2), :]
                lhs[:, (2 * j + half) * LANES : (2 * j + half + 1) * LANES] = values.astype(jnp.bfloat16)

    def product(turn):
        at = pl.multiple_of(turn * (group * wide), group * wide)
        return lax.dot_general(
            weights[:, pl.ds(at, group * wide)],
            lhs[...],
            (((1,), (1,)), ((), ())),
            preferred_element_type=jnp.float32,
        )

    @pl.when(block == 0)
    def _():
        for part, ref in enumerate((low_ref, mid_ref, high_ref)):
            @pl.loop(0, leaves // rows)
            def _(chunk):
                values = ref[pl.ds(chunk * rows, rows), :].astype(jnp.float32)
                lane_halves(source, 2 * (part * leaves + chunk * rows), values)

    pick(0)
    settle()

    @pl.when(block == 0)
    def _():
        for tap in range(taps):
            weights[:, tap * wide + LANES : (tap + 1) * wide] = jnp.zeros((weights.shape[0], LANES), weights.dtype)
            weights[:, tap * wide : tap * wide + depth] = ops_ref[tap]

    out_ref[...] = jnp.zeros_like(out_ref)

    @pl.loop(0, taps // group - 1)
    def _(turn):
        out_ref[...] += product(turn)
        pick(turn + 1)
        settle()

    out_ref[...] += product(taps // group - 1)


def near_field(low, mid, high, local_rows, near_ops):
    leaves = mid.shape[0]
    taps, depth, outs = near_ops.shape
    rows = 256 if leaves % 256 == 0 else leaves
    group = 3 if taps % 3 == 0 else 1
    flat = local_rows.T.reshape(-1)
    vmem = pl.BlockSpec(memory_space=pltpu.VMEM)
    return pl.pallas_call(
        functools.partial(near_kernel, rows, group),
        out_shape=jax.ShapeDtypeStruct((outs, leaves), jnp.float32),
        grid=(leaves // rows,),
        in_specs=[pl.BlockSpec(memory_space=pltpu.SMEM), vmem, vmem, vmem, vmem],
        out_specs=pl.BlockSpec((outs, rows), lambda i: (0, i)),
        scratch_shapes=[
            pltpu.VMEM((3 * leaves, 2, LANES), jnp.float32),
            pltpu.VMEM((group * rows, 2, LANES), jnp.float32),
            pltpu.VMEM((rows, group * 2 * LANES), jnp.bfloat16),
            pltpu.VMEM((outs, taps * 2 * LANES), jnp.bfloat16),
        ],
        compiler_params=pltpu.CompilerParams(
            dimension_semantics=("arbitrary",), vmem_limit_bytes=36 * 1024 * 1024
        ),
        cost_estimate=pl.CostEstimate(
            flops=2 * leaves * taps * 2 * LANES * outs * 5, bytes_accessed=100_000_000, transcendentals=0
        ),
        name="near_field",
    )(flat, low, mid, high, near_ops.transpose(0, 2, 1))


def base_kernel(
    rows, n, idx_ref, field_ref, class_ref, ops_ref, carried_ref, wide_ref, out_ref, low_ref, high_ref,
    source, picked, lhs, weights, send_sem, recv_sem,
):
    me = lax.axis_index("leaf")
    right, left = lax.rem(me + 1, n), lax.rem(me + n - 1, n)
    kinds, depth, outs = ops_ref.shape
    wide = 2 * LANES
    slots = field_ref.shape[0]
    capacity = carried_ref.shape[0]
    barrier = pltpu.get_barrier_semaphore()
    for neighbour in (left, right):
        pl.semaphore_signal(barrier, inc=1, device_id=(neighbour,), device_id_type=MESH)

    @pl.loop(0, slots // rows)
    def _(chunk):
        values = field_ref[pl.ds(chunk * rows, rows), :].astype(jnp.float32)
        lane_halves(source, 2 * chunk * rows, values)

    pl.semaphore_wait(barrier, 2)
    copies = [
        pltpu.make_async_remote_copy(
            src_ref=wide_ref,
            dst_ref=landing,
            send_sem=send_sem.at[which],
            recv_sem=recv_sem.at[which],
            device_id=(neighbour,),
            device_id_type=MESH,
        )
        for which, (landing, neighbour) in enumerate(((low_ref, right), (high_ref, left)))
    ]
    for copy in copies:
        copy.start()

    for kind in range(kinds):
        weights[kind * wide : (kind + 1) * wide, LANES:] = jnp.zeros((wide, LANES), weights.dtype)
        weights[kind * wide : (kind + 1) * wide, :outs] = jnp.concatenate(
            [ops_ref[kind], jnp.zeros((wide - depth, outs), ops_ref.dtype)], axis=0
        )
    extra = jnp.concatenate([carried_ref[...].astype(jnp.float32)] * (rows // capacity), axis=0)

    @pl.loop(0, slots // rows)
    def _(block):
        for r in range(rows):
            picked[r] = source[idx_ref[block * rows + r]]
        flat = picked.reshape(2 * rows, LANES)
        halves = [flat[pl.ds(half, rows, stride=2), :] for half in range(2)]
        here = pl.ds(pl.multiple_of(block * rows, rows), rows)
        classes = class_ref[here, :]
        for kind in range(kinds):
            for half in range(2):
                at = kind * wide + half * LANES
                lhs[:, at : at + LANES] = jnp.where(classes == kind, halves[half], 0.0).astype(jnp.bfloat16)
        total = jnp.dot(lhs[...], weights[...], preferred_element_type=jnp.float32)
        out_ref[here, :] = (total + extra).astype(jnp.bfloat16)

    for copy in copies:
        copy.wait()


def base_rows(concentration, departure, departure_class, shift_ops, carried, own):
    slots, _ = concentration.shape
    capacity = carried.shape[0]
    kinds = shift_ops.shape[0]
    rows = 256 if slots % 256 == 0 and 256 % capacity == 0 else slots
    wide = 2 * LANES
    vmem = pl.BlockSpec(memory_space=pltpu.VMEM)
    return pl.pallas_call(
        functools.partial(base_kernel, rows, slots // capacity),
        out_shape=(
            jax.ShapeDtypeStruct((slots, wide), jnp.bfloat16),
            jax.ShapeDtypeStruct(own.shape, jnp.bfloat16),
            jax.ShapeDtypeStruct(own.shape, jnp.bfloat16),
        ),
        in_specs=[pl.BlockSpec(memory_space=pltpu.SMEM)] + [vmem] * 5,
        out_specs=(vmem, vmem, vmem),
        scratch_shapes=[
            pltpu.VMEM((slots, 2, LANES), jnp.float32),
            pltpu.VMEM((rows, 2, LANES), jnp.float32),
            pltpu.VMEM((rows, kinds * wide), jnp.bfloat16),
            pltpu.VMEM((kinds * wide, wide), jnp.bfloat16),
            pltpu.SemaphoreType.DMA((2,)),
            pltpu.SemaphoreType.DMA((2,)),
        ],
        compiler_params=pltpu.CompilerParams(
            collective_id=1, has_side_effects=True, vmem_limit_bytes=24 * 1024 * 1024
        ),
        cost_estimate=pl.CostEstimate(
            flops=2 * slots * kinds * wide * wide, bytes_accessed=4 * slots * wide, transcendentals=0
        ),
        name="base_rows",
    )(departure, concentration, departure_class[:, None], shift_ops, carried, own)


def shift_of(turn, n):
    half = lax.div(turn + 1, 2)
    return lax.rem(n // 2 + n + jnp.where(lax.rem(turn, 2) == 1, half, -half), n)


def turn_of(shift, n):
    apart = lax.rem(shift + n - n // 2, n)
    return jnp.where(apart == 0, 0, jnp.where(apart <= n // 2, 2 * apart - 1, 2 * (n - apart)))


def return_kernel(
    n, group, slot_ref, alive_ref, near_ref, far_ref, got_ref, eval_ref, vel_ref, adv_ref,
    moved, spread, spread_low, values_op, result, send_sem, recv_sem,
):
    me = lax.axis_index("leaf")
    capacity, wide = got_ref.shape[1], got_ref.shape[2]
    depth, nodes = eval_ref.shape[0], eval_ref.shape[1] // 4
    outs, leaves = near_ref.shape
    padded = moved.shape[0]
    rows = group * capacity
    barrier = pltpu.get_barrier_semaphore()

    @pl.loop(1, n)
    def _(turn):
        pl.semaphore_signal(barrier, inc=1, device_id=(lax.rem(me + turn, n),), device_id_type=MESH)

    far = far_ref[...]
    for at in range(0, leaves, LANES):
        block = ((near_ref[:, at : at + LANES] + far) * alive_ref[:, at : at + LANES]).astype(jnp.bfloat16)
        vel_ref[:, at : at + LANES] = block
        moved[:, at : at + LANES] = jnp.concatenate(
            [block, jnp.ones((padded - outs, LANES), jnp.bfloat16)], axis=0
        )
    spread[...] = jnp.zeros_like(spread)
    for j in range(3):
        spread[j * depth : (j + 1) * depth, j * nodes : (j + 1) * nodes] = eval_ref[:, :nodes].astype(jnp.float32)
    spread_low[...] = spread[...].astype(jnp.bfloat16)
    values_op[...] = jnp.concatenate(
        [eval_ref[...], jnp.zeros((wide - depth, 4 * nodes), jnp.bfloat16)], axis=0
    )
    pl.semaphore_wait(barrier, n - 1)

    def copy(turn, landing):
        return pltpu.make_async_remote_copy(
            src_ref=result.at[turn],
            dst_ref=adv_ref.at[landing],
            send_sem=send_sem.at[turn],
            recv_sem=recv_sem.at[turn],
            device_id=(lax.rem(me + shift_of(turn, n), n),),
            device_id_type=MESH,
        )

    @pl.loop(0, n // group)
    def _(step):
        ids = lax.broadcasted_iota(jnp.int32, (rows, 1), 0) + step * rows
        placed = jnp.where(slot_ref[...] == ids, 1.0, 0.0).astype(jnp.bfloat16)
        sent = lax.dot_general(
            placed, moved[...], (((1,), (1,)), ((), ())), preferred_element_type=jnp.float32
        )
        speeds = jnp.dot(sent.astype(jnp.bfloat16), spread_low[...], preferred_element_type=jnp.float32)
        base = jnp.concatenate(
            [got_ref[lax.rem(me + shift_of(step * group + j, n), n)] for j in range(group)], axis=0
        )
        values = jnp.dot(base, values_op[...], preferred_element_type=jnp.float32)
        correction = speeds[:, :nodes] * values[:, nodes : 2 * nodes]
        correction = correction + speeds[:, nodes : 2 * nodes] * values[:, 2 * nodes : 3 * nodes]
        correction = correction + speeds[:, 2 * nodes :] * values[:, 3 * nodes :]
        filled = sent[:, outs : outs + 1]
        final = (filled * (values[:, :nodes] - time_step * correction)).astype(jnp.bfloat16)
        for j in range(group):
            result[step * group + j] = final[j * capacity : (j + 1) * capacity]
        for j in range(group):
            if j < group - 1:
                copy(step * group + j, me).start()
            else:
                @pl.when(step < n // group - 1)
                def _():
                    copy(step * group + group - 1, me).start()

    adv_ref[me] = result[n - 1]

    @pl.loop(0, n - 1)
    def _(turn):
        copy(turn, lax.rem(me - shift_of(turn, n) + n, n)).wait()


def advect_return(slot, alive, near, far, got, eval_ops):
    n, capacity, wide = got.shape
    depth, columns = eval_ops.shape
    outs, leaves = near.shape
    nodes = columns // 4
    group = 256 // capacity if 256 % capacity == 0 and n % (256 // capacity) == 0 else 1
    padded = -(-(outs + 1) // (2 * LANES)) * (2 * LANES)
    vmem = pl.BlockSpec(memory_space=pltpu.VMEM)
    return pl.pallas_call(
        functools.partial(return_kernel, n, group),
        out_shape=(
            jax.ShapeDtypeStruct((outs, leaves), jnp.bfloat16),
            jax.ShapeDtypeStruct((n, capacity, nodes), jnp.bfloat16),
        ),
        in_specs=[vmem] * 6,
        out_specs=(vmem, vmem),
        scratch_shapes=[
            pltpu.VMEM((padded, leaves), jnp.bfloat16),
            pltpu.VMEM((padded, 3 * nodes), jnp.float32),
            pltpu.VMEM((padded, 3 * nodes), jnp.bfloat16),
            pltpu.VMEM((wide, columns), jnp.bfloat16),
            pltpu.VMEM((n, capacity, nodes), jnp.bfloat16),
            pltpu.SemaphoreType.DMA((n,)),
            pltpu.SemaphoreType.DMA((n,)),
        ],
        compiler_params=pltpu.CompilerParams(
            collective_id=0, has_side_effects=True, vmem_limit_bytes=24 * 1024 * 1024
        ),
        cost_estimate=pl.CostEstimate(
            flops=2 * n * capacity * (leaves * padded + padded * 3 * nodes + wide * columns),
            bytes_accessed=10_000_000,
            transcendentals=0,
        ),
        name="advect_return",
    )(slot, alive, near, far, got, eval_ops)


def rounded(values):
    return lax.reduce_precision(values, exponent_bits=8, mantissa_bits=7)


def split3(values):
    high = rounded(values)
    middle = rounded(values - high)
    low = rounded(values - high - middle)
    return jnp.stack([high, middle, low], axis=-1).astype(jnp.bfloat16)


def local(
    density,
    vel_mask,
    near_list,
    near_ops,
    upward_ops,
    coupling_operators,
    coarse_weights,
    downward_ops,
    conc_owner,
    concentration,
    departure,
    departure_class,
    shift_ops,
    eval_ops,
):
    leaves = density.shape[0]
    coef_width = density.shape[1]
    devices = lax.axis_size("leaf")
    my_index = lax.axis_index("leaf")
    alive = vel_mask.astype(jnp.float32)
    live_density = (density.astype(jnp.float32) * alive[:, None]).astype(jnp.bfloat16)
    wide = jnp.pad(live_density, ((0, 0), (0, 2 * LANES - coef_width)))
    parts = jnp.einsum(
        "gop,opq->goq",
        live_density.reshape(-1, 8, coef_width),
        upward_ops,
        preferred_element_type=jnp.float32,
    )
    own_part = jnp.sum(parts, axis=(0, 1))
    slots_here = concentration.shape[0]
    capacity = slots_here // devices
    densities = own_part.shape[0]
    columns = -(-densities // capacity)
    carried = split3(jnp.pad(own_part, (0, columns * capacity - densities)))
    carried = jnp.pad(
        carried.reshape(capacity, 3 * columns),
        ((0, 0), (coef_width, 2 * LANES - coef_width - 3 * columns)),
    )
    base, low, high = base_rows(concentration, departure, departure_class, shift_ops, carried, wide)
    local_rows = near_list - my_index * leaves + leaves
    nearby_field = near_field(low, wide, high, local_rows, near_ops)
    got = lax.all_to_all(
        base.reshape(devices, capacity, -1), "leaf", split_axis=0, concat_axis=0, tiled=True
    )
    all_parts = jnp.sum(
        got[:, :, coef_width : coef_width + 3 * columns]
        .astype(jnp.float32)
        .reshape(devices, columns * capacity, 3),
        axis=2,
    )[:, :densities]
    moments = jnp.sum(all_parts.reshape(devices // SPAN, SPAN, densities), axis=1)
    my_box = my_index // SPAN
    expanded = jnp.dot(moments, coupling_operators, precision=lax.Precision.HIGHEST)
    weight_row = lax.dynamic_slice_in_dim(coarse_weights, my_box, 1, 0)
    own_expansion = jnp.dot(weight_row, expanded, precision=lax.Precision.HIGHEST)
    box_far = jnp.einsum(
        "jq,oqp->jpo",
        own_expansion.reshape(3, -1),
        downward_ops.astype(jnp.float32),
        precision=lax.Precision.HIGHEST,
    )
    far = jnp.tile(box_far.reshape(3 * coef_width, 8), (1, LANES // 8))
    owner = conc_owner[:, 0]
    onehot = owner[:, None] == jnp.arange(devices, dtype=jnp.int32)[None, :]
    order = jnp.arange(leaves, dtype=jnp.int32)
    earlier = (order[None, :] < order[:, None]).astype(jnp.bfloat16)
    before = jnp.dot(earlier, onehot.astype(jnp.bfloat16), preferred_element_type=jnp.float32)
    rank = jnp.sum(jnp.where(onehot, before, 0.0), axis=1).astype(jnp.int32)
    relative = lax.rem(owner - my_index + devices, devices)
    send_slot = jnp.where(vel_mask > 0, turn_of(relative, devices) * capacity + rank, -1)
    velocity, advected = advect_return(
        send_slot[None, :], alive[None, :], nearby_field, far, got, eval_ops
    )
    return (velocity.T, advected.reshape(slots_here, -1))


def solution(mesh):
    placed = (
        P("leaf", None),
        P("leaf"),
        P("leaf", None),
        P(),
        P(),
        P(),
        P(),
        P(),
        P("leaf", None),
        P("leaf", None),
        P("leaf"),
        P("leaf"),
        P(),
        P(),
    )
    return jax.shard_map(
        local,
        mesh=mesh,
        in_specs=placed,
        out_specs=(P("leaf", None), P("leaf", None)),
        check_vma=False,
    )
```

```python
import functools

import jax
import jax.numpy as jnp
from jax import lax
from jax.experimental import pallas as pl
from jax.experimental.pallas import tpu as pltpu
from jax.sharding import PartitionSpec as P

SPAN = 4


time_step = 0.5


LANES = 128


def halo(block):
    count = lax.axis_size("leaf")
    forward = [(i, i + 1) for i in range(count - 1)]
    backward = [(target, source) for source, target in forward]
    return lax.ppermute(block, "leaf", forward), lax.ppermute(block, "leaf", backward)


MARGIN = 8


def lane_halves(low, high, at, values):
    count, width = values.shape
    low[pl.ds(at, count), :] = values[:, :LANES]
    upper = values[:, LANES:]
    if width < 2 * LANES:
        upper = jnp.concatenate([upper, jnp.zeros((count, 2 * LANES - width), values.dtype)], axis=1)
    high[pl.ds(at, count), :] = upper


def starts_of(rows):
    spread = jnp.arange(rows.shape[-1], dtype=jnp.int32) % MARGIN
    return rows + (MARGIN - spread)


def gather_groups(sources, starts_ref, at, rows):
    sublane = lax.broadcasted_iota(jnp.int32, (MARGIN, LANES), 0)
    bits = [lax.rem(lax.div(sublane, 1 << bit), 2) == 1 for bit in range(3)]
    for first in range(0, rows, 2 * MARGIN):
        parts = [[], []]
        for group in range(first, first + 2 * MARGIN, MARGIN):
            starts = [starts_ref[at + group + k] for k in range(MARGIN)]
            for part, source in zip(parts, sources):
                loads = [source[pl.ds(start, MARGIN), :] for start in starts]
                for bit in bits:
                    loads = [jnp.where(bit, b, a) for a, b in zip(loads[::2], loads[1::2])]
                part.append(loads[0])
        yield first, [jnp.concatenate(part, axis=0) for part in parts]


def near_kernel(
    rows, group, idx_ref, low_ref, mid_ref, high_ref, ops_ref, out_ref,
    source_low, source_high, lhs_even, lhs_odd, raw, weights, sem,
):
    block = pl.program_id(0)
    taps, _, depth = ops_ref.shape
    wide = 2 * LANES
    leaves = mid_ref.shape[0]
    turns = taps // group
    fetch = pltpu.make_async_copy(ops_ref, raw, sem)

    def pick(turn, lhs):
        for j in range(group):
            at = (turn * group + j) * leaves + block * rows
            for first, halves in gather_groups((source_low, source_high), idx_ref, at, rows):
                for half, values in enumerate(halves):
                    column = (2 * j + half) * LANES
                    lhs[first : first + 2 * MARGIN, column : column + LANES] = values.astype(jnp.bfloat16)

    def product(turn, lhs):
        at = pl.multiple_of(turn * (group * wide), group * wide)
        return lax.dot_general(
            weights[:, pl.ds(at, group * wide)],
            lhs[...],
            (((1,), (1,)), ((), ())),
            preferred_element_type=jnp.float32,
        )

    @pl.when(block == 0)
    def _():
        fetch.start()
        for part, ref in enumerate((low_ref, mid_ref, high_ref)):
            @pl.loop(0, leaves // rows)
            def _(chunk):
                values = ref[pl.ds(chunk * rows, rows), :].astype(jnp.float32)
                lane_halves(source_low, source_high, MARGIN + part * leaves + chunk * rows, values)

    pick(0, lhs_even)

    @pl.when(block == 0)
    def _():
        fetch.wait()
        for tap in range(taps):
            weights[:, tap * wide + LANES : (tap + 1) * wide] = jnp.zeros((weights.shape[0], LANES), weights.dtype)
            weights[:, tap * wide : tap * wide + depth] = raw[tap]

    out_ref[...] = jnp.zeros_like(out_ref)

    @pl.loop(0, (turns - 1) // 2)
    def _(pair):
        turn = 2 * pair
        out_ref[...] += product(turn, lhs_even)
        pick(turn + 1, lhs_odd)
        out_ref[...] += product(turn + 1, lhs_odd)
        pick(turn + 2, lhs_even)

    if turns % 2 == 0:
        out_ref[...] += product(turns - 2, lhs_even)
        pick(turns - 1, lhs_odd)
        out_ref[...] += product(turns - 1, lhs_odd)
    else:
        out_ref[...] += product(turns - 1, lhs_even)


def near_field(low, mid, high, local_rows, near_ops):
    leaves = mid.shape[0]
    taps, depth, outs = near_ops.shape
    rows = 256 if leaves % 256 == 0 else leaves
    group = 3 if taps % 3 == 0 else 1
    flat = starts_of(local_rows.T).reshape(-1)
    vmem = pl.BlockSpec(memory_space=pltpu.VMEM)
    return pl.pallas_call(
        functools.partial(near_kernel, rows, group),
        out_shape=jax.ShapeDtypeStruct((outs, leaves), jnp.float32),
        grid=(leaves // rows,),
        in_specs=[
            pl.BlockSpec(memory_space=pltpu.SMEM), vmem, vmem, vmem, pl.BlockSpec(memory_space=pl.ANY)
        ],
        out_specs=pl.BlockSpec((outs, rows), lambda i: (0, i)),
        scratch_shapes=[
            pltpu.VMEM((3 * leaves + 2 * MARGIN, LANES), jnp.float32),
            pltpu.VMEM((3 * leaves + 2 * MARGIN, LANES), jnp.float32),
            pltpu.VMEM((rows, group * 2 * LANES), jnp.bfloat16),
            pltpu.VMEM((rows, group * 2 * LANES), jnp.bfloat16),
            pltpu.VMEM((taps, outs, depth), jnp.bfloat16),
            pltpu.VMEM((outs, taps * 2 * LANES), jnp.bfloat16),
            pltpu.SemaphoreType.DMA(()),
        ],
        compiler_params=pltpu.CompilerParams(
            dimension_semantics=("arbitrary",), vmem_limit_bytes=60 * 1024 * 1024
        ),
        cost_estimate=pl.CostEstimate(
            flops=2 * leaves * taps * 2 * LANES * outs * 5, bytes_accessed=100_000_000, transcendentals=0
        ),
        name="near_field",
    )(flat, low, mid, high, near_ops.transpose(0, 2, 1))


def base_kernel(rows, capacity, idx_ref, field_ref, class_ref, ops_ref, carried_ref, out_ref, source_low, source_high, lhs, weights):
    block = pl.program_id(0)
    kinds, depth, outs = ops_ref.shape
    wide = 2 * LANES

    @pl.when(block == 0)
    def _():
        @pl.loop(0, field_ref.shape[0] // rows)
        def _(chunk):
            values = field_ref[pl.ds(chunk * rows, rows), :].astype(jnp.float32)
            lane_halves(source_low, source_high, MARGIN + chunk * rows, values)

        for kind in range(kinds):
            weights[kind * wide : (kind + 1) * wide, LANES:] = jnp.zeros((wide, LANES), weights.dtype)
            weights[kind * wide : (kind + 1) * wide, :outs] = jnp.concatenate(
                [ops_ref[kind], jnp.zeros((wide - depth, outs), ops_ref.dtype)], axis=0
            )

    for first, halves in gather_groups((source_low, source_high), idx_ref, block * rows, rows):
        here = slice(first, first + 2 * MARGIN)
        classes = class_ref[here, :]
        for kind in range(kinds):
            chosen = classes == kind
            for half, values in enumerate(halves):
                at = kind * wide + half * LANES
                lhs[here, at : at + LANES] = jnp.where(chosen, values, 0.0).astype(jnp.bfloat16)
    total = jnp.dot(lhs[...], weights[...], preferred_element_type=jnp.float32)
    extra = carried_ref[...].astype(jnp.float32)
    out_ref[...] = (total + jnp.concatenate([extra] * (rows // capacity), axis=0)).astype(jnp.bfloat16)


def base_rows(concentration, departure, departure_class, shift_ops, carried):
    slots, width = concentration.shape
    capacity = carried.shape[0]
    kinds = shift_ops.shape[0]
    rows = 256 if slots % 256 == 0 and 256 % capacity == 0 else slots
    wide = 2 * LANES
    vmem = pl.BlockSpec(memory_space=pltpu.VMEM)
    return pl.pallas_call(
        functools.partial(base_kernel, rows, capacity),
        out_shape=jax.ShapeDtypeStruct((slots, wide), jnp.bfloat16),
        grid=(slots // rows,),
        in_specs=[
            pl.BlockSpec(memory_space=pltpu.SMEM),
            vmem,
            pl.BlockSpec((rows, 1), lambda i: (i, 0)),
            vmem,
            vmem,
        ],
        out_specs=pl.BlockSpec((rows, wide), lambda i: (i, 0)),
        scratch_shapes=[
            pltpu.VMEM((slots + 2 * MARGIN, LANES), jnp.float32),
            pltpu.VMEM((slots + 2 * MARGIN, LANES), jnp.float32),
            pltpu.VMEM((rows, kinds * wide), jnp.bfloat16),
            pltpu.VMEM((kinds * wide, wide), jnp.bfloat16),
        ],
        compiler_params=pltpu.CompilerParams(
            dimension_semantics=("arbitrary",), vmem_limit_bytes=32 * 1024 * 1024
        ),
        cost_estimate=pl.CostEstimate(
            flops=2 * slots * kinds * wide * wide, bytes_accessed=4 * slots * wide, transcendentals=0
        ),
        name="base_rows",
    )(starts_of(departure), concentration, departure_class[:, None], shift_ops, carried)


MESH = pl.DeviceIdType.MESH


def shift_of(turn, n):
    half = lax.div(turn + 1, 2)
    return lax.rem(n // 2 + n + jnp.where(lax.rem(turn, 2) == 1, half, -half), n)


def turn_of(shift, n):
    apart = lax.rem(shift + n - n // 2, n)
    return jnp.where(apart == 0, 0, jnp.where(apart <= n // 2, 2 * apart - 1, 2 * (n - apart)))


def return_kernel(
    n, group, slot_ref, alive_ref, near_ref, far_ref, got_ref, eval_ref, vel_ref, adv_ref,
    moved, spread, spread_low, values_op, result, send_sem, recv_sem,
):
    me = lax.axis_index("leaf")
    capacity, wide = got_ref.shape[1], got_ref.shape[2]
    depth, nodes = eval_ref.shape[0], eval_ref.shape[1] // 4
    outs, leaves = near_ref.shape
    padded = moved.shape[0]
    rows = group * capacity
    barrier = pltpu.get_barrier_semaphore()

    @pl.loop(1, n)
    def _(turn):
        pl.semaphore_signal(barrier, inc=1, device_id=(lax.rem(me + turn, n),), device_id_type=MESH)

    far = far_ref[...]
    for at in range(0, leaves, LANES):
        block = ((near_ref[:, at : at + LANES] + far) * alive_ref[:, at : at + LANES]).astype(jnp.bfloat16)
        vel_ref[:, at : at + LANES] = block
        moved[:, at : at + LANES] = jnp.concatenate(
            [block, jnp.ones((padded - outs, LANES), jnp.bfloat16)], axis=0
        )
    spread[...] = jnp.zeros_like(spread)
    for j in range(3):
        spread[j * depth : (j + 1) * depth, j * nodes : (j + 1) * nodes] = eval_ref[:, :nodes].astype(jnp.float32)
    spread_low[...] = spread[...].astype(jnp.bfloat16)
    values_op[...] = jnp.concatenate(
        [eval_ref[...], jnp.zeros((wide - depth, 4 * nodes), jnp.bfloat16)], axis=0
    )
    pl.semaphore_wait(barrier, n - 1)

    def copy(turn, landing):
        return pltpu.make_async_remote_copy(
            src_ref=result.at[turn],
            dst_ref=adv_ref.at[landing],
            send_sem=send_sem.at[turn],
            recv_sem=recv_sem.at[turn],
            device_id=(lax.rem(me + shift_of(turn, n), n),),
            device_id_type=MESH,
        )

    @pl.loop(0, n // group)
    def _(step):
        ids = lax.broadcasted_iota(jnp.int32, (rows, 1), 0) + step * rows
        placed = jnp.where(slot_ref[...] == ids, 1.0, 0.0).astype(jnp.bfloat16)
        sent = lax.dot_general(
            placed, moved[...], (((1,), (1,)), ((), ())), preferred_element_type=jnp.float32
        )
        speeds = jnp.dot(sent.astype(jnp.bfloat16), spread_low[...], preferred_element_type=jnp.float32)
        base = jnp.concatenate(
            [got_ref[lax.rem(me + shift_of(step * group + j, n), n)] for j in range(group)], axis=0
        )
        values = jnp.dot(base, values_op[...], preferred_element_type=jnp.float32)
        correction = speeds[:, :nodes] * values[:, nodes : 2 * nodes]
        correction = correction + speeds[:, nodes : 2 * nodes] * values[:, 2 * nodes : 3 * nodes]
        correction = correction + speeds[:, 2 * nodes :] * values[:, 3 * nodes :]
        filled = sent[:, outs : outs + 1]
        final = (filled * (values[:, :nodes] - time_step * correction)).astype(jnp.bfloat16)
        for j in range(group):
            result[step * group + j] = final[j * capacity : (j + 1) * capacity]
        for j in range(group):
            if j < group - 1:
                copy(step * group + j, me).start()
            else:
                @pl.when(step < n // group - 1)
                def _():
                    copy(step * group + group - 1, me).start()

    adv_ref[me] = result[n - 1]

    @pl.loop(0, n - 1)
    def _(turn):
        copy(turn, lax.rem(me - shift_of(turn, n) + n, n)).wait()


def advect_return(slot, alive, near, far, got, eval_ops):
    n, capacity, wide = got.shape
    depth, columns = eval_ops.shape
    outs, leaves = near.shape
    nodes = columns // 4
    group = 256 // capacity if 256 % capacity == 0 and n % (256 // capacity) == 0 else 1
    padded = -(-(outs + 1) // (2 * LANES)) * (2 * LANES)
    vmem = pl.BlockSpec(memory_space=pltpu.VMEM)
    return pl.pallas_call(
        functools.partial(return_kernel, n, group),
        out_shape=(
            jax.ShapeDtypeStruct((outs, leaves), jnp.bfloat16),
            jax.ShapeDtypeStruct((n, capacity, nodes), jnp.bfloat16),
        ),
        in_specs=[vmem] * 6,
        out_specs=(vmem, vmem),
        scratch_shapes=[
            pltpu.VMEM((padded, leaves), jnp.bfloat16),
            pltpu.VMEM((padded, 3 * nodes), jnp.float32),
            pltpu.VMEM((padded, 3 * nodes), jnp.bfloat16),
            pltpu.VMEM((wide, columns), jnp.bfloat16),
            pltpu.VMEM((n, capacity, nodes), jnp.bfloat16),
            pltpu.SemaphoreType.DMA((n,)),
            pltpu.SemaphoreType.DMA((n,)),
        ],
        compiler_params=pltpu.CompilerParams(
            collective_id=0, has_side_effects=True, vmem_limit_bytes=48 * 1024 * 1024
        ),
        cost_estimate=pl.CostEstimate(
            flops=2 * n * capacity * (leaves * padded + padded * 3 * nodes + wide * columns),
            bytes_accessed=10_000_000,
            transcendentals=0,
        ),
        name="advect_return",
    )(slot, alive, near, far, got, eval_ops)


def rounded(values):
    return lax.reduce_precision(values, exponent_bits=8, mantissa_bits=7)


def split3(values):
    high = rounded(values)
    middle = rounded(values - high)
    low = rounded(values - high - middle)
    return jnp.stack([high, middle, low], axis=-1).astype(jnp.bfloat16)


def local(
    density,
    vel_mask,
    near_list,
    near_ops,
    upward_ops,
    coupling_operators,
    coarse_weights,
    downward_ops,
    conc_owner,
    concentration,
    departure,
    departure_class,
    shift_ops,
    eval_ops,
):
    leaves = density.shape[0]
    coef_width = density.shape[1]
    devices = lax.axis_size("leaf")
    my_index = lax.axis_index("leaf")
    alive = vel_mask.astype(jnp.float32)
    live_density = (density.astype(jnp.float32) * alive[:, None]).astype(jnp.bfloat16)
    wide = jnp.pad(live_density, ((0, 0), (0, 2 * LANES - coef_width)))
    low, high = halo(wide)
    local_rows = near_list - my_index * leaves + leaves
    nearby_field = near_field(low, wide, high, local_rows, near_ops)
    parts = jnp.einsum(
        "gop,opq->goq",
        live_density.reshape(-1, 8, coef_width),
        upward_ops,
        preferred_element_type=jnp.float32,
    )
    own_part = jnp.sum(parts, axis=(0, 1))
    slots_here = concentration.shape[0]
    capacity = slots_here // devices
    densities = own_part.shape[0]
    columns = -(-densities // capacity)
    carried = split3(jnp.pad(own_part, (0, columns * capacity - densities)))
    carried = jnp.pad(
        carried.reshape(capacity, 3 * columns),
        ((0, 0), (coef_width, 2 * LANES - coef_width - 3 * columns)),
    )
    base = base_rows(concentration, departure, departure_class, shift_ops, carried)
    got = lax.all_to_all(
        base.reshape(devices, capacity, -1), "leaf", split_axis=0, concat_axis=0, tiled=True
    )
    all_parts = jnp.sum(
        got[:, :, coef_width : coef_width + 3 * columns]
        .astype(jnp.float32)
        .reshape(devices, columns * capacity, 3),
        axis=2,
    )[:, :densities]
    moments = jnp.sum(all_parts.reshape(devices // SPAN, SPAN, densities), axis=1)
    my_box = my_index // SPAN
    expanded = jnp.dot(moments, coupling_operators, precision=lax.Precision.HIGHEST)
    weight_row = lax.dynamic_slice_in_dim(coarse_weights, my_box, 1, 0)
    own_expansion = jnp.dot(weight_row, expanded, precision=lax.Precision.HIGHEST)
    box_far = jnp.einsum(
        "jq,oqp->jpo",
        own_expansion.reshape(3, -1),
        downward_ops.astype(jnp.float32),
        precision=lax.Precision.HIGHEST,
    )
    far = jnp.tile(box_far.reshape(3 * coef_width, 8), (1, LANES // 8))
    owner = conc_owner[:, 0]
    onehot = owner[:, None] == jnp.arange(devices, dtype=jnp.int32)[None, :]
    order = jnp.arange(leaves, dtype=jnp.int32)
    earlier = (order[None, :] < order[:, None]).astype(jnp.bfloat16)
    before = jnp.dot(earlier, onehot.astype(jnp.bfloat16), preferred_element_type=jnp.float32)
    rank = jnp.sum(jnp.where(onehot, before, 0.0), axis=1).astype(jnp.int32)
    relative = lax.rem(owner - my_index + devices, devices)
    send_slot = jnp.where(vel_mask > 0, turn_of(relative, devices) * capacity + rank, -1)
    velocity, advected = advect_return(
        send_slot[None, :], alive[None, :], nearby_field, far, got, eval_ops
    )
    return (velocity.T, advected.reshape(slots_here, -1))


def solution(mesh):
    placed = (
        P("leaf", None),
        P("leaf"),
        P("leaf", None),
        P(),
        P(),
        P(),
        P(),
        P(),
        P("leaf", None),
        P("leaf", None),
        P("leaf"),
        P("leaf"),
        P(),
        P(),
    )
    return jax.shard_map(
        local,
        mesh=mesh,
        in_specs=placed,
        out_specs=(P("leaf", None), P("leaf", None)),
        check_vma=False,
    )
```
